32 devices in a mesh: groups: 2 (over x), blk: 8 (over z, y), docs: 2 (over core).
Axes of the slice: x: 2, y: 2, z: 4, core: 2. Of those that a mesh axis runs over, the one named last changes fastest.
Arguments:
- queries: bfloat16 [128, 2048], P(('groups', 'blk')), parts along dimension 0, may hold values from -6 to 6
- whiten: bfloat16 [4096, 2048], P(('groups', 'blk', 'docs')), parts along dimension 0, may hold values from -1 to 2
- documents: float32 [32768, 2048], P(('groups', 'blk', 'docs')), parts along dimension 0, may hold values from -600 to 600
Outputs:
- standardized: float32 [128, 16384], P('groups', ('blk', 'docs')), parts along dimension 0
The draws below stay inside these ranges and needn't reach their ends.
There are 2 independent parts, one for each index of `groups`. The reference program is written for one: setup_inputs(seed, part) draws one part's arguments, and reference() takes and returns one part's arrays. A program takes and returns all parts, laid end to end along the dimension named above; each array names one. Nothing has to cross between parts.
All inputs are finite; a program needn't handle non-finite values.
Results may differ from the reference program's by a relative error of at most 0.0003.
Values may be sent and summed in bfloat16 or wider, within the bound.
A program may use at most 64 MiB of HBM per device.

```python
import math
import jax
import jax.numpy as jnp
from jax import lax

K = 2048
NQ = 64
NDOC = 16384


def draw_whiten(key, part):
    key = jax.random.fold_in(key, 12)
    noise = jnp.clip(jax.random.normal(key, (K, K), jnp.float32), -6.0, 6.0)
    matrix = jnp.eye(K, dtype=jnp.float32) + 0.7 * noise / math.sqrt(K)
    return matrix.astype(jnp.bfloat16)


def draw_documents(key, part):
    key = jax.random.fold_in(key, 11)
    key_noise, key_rows, key_cols, key_common = jax.random.split(key, 4)
    noise = jnp.clip(jax.random.normal(key_noise, (NDOC, K), jnp.float32), -6.0, 6.0)
    trend = 1.0 + 2.0 * jnp.arange(NDOC, dtype=jnp.float32) / NDOC
    rows = jnp.exp(jax.random.uniform(key_rows, (NDOC, 1), jnp.float32) * math.log(10.0)) * trend[:, None]
    cols = jnp.exp(jax.random.uniform(key_cols, (1, K), jnp.float32) * math.log(10.0)) / 10.0
    common_dir = jnp.clip(jax.random.normal(key_common, (1, K), jnp.float32), -4.0, 4.0)
    weight = 1.5
    return (rows * (noise * cols + weight * common_dir)).astype(jnp.float32)


def block_levels(own_key, dims, pieces, least, high):
    def one(dim, blocks):
        steps = jax.random.uniform(jax.random.fold_in(jax.random.fold_in(own_key, 6), dim), (blocks,), jnp.float32, least / len(pieces), high / len(pieces))
        return jnp.repeat(jnp.exp(steps), dims[dim] // blocks).reshape((-1,) + (1,) * (len(dims) - dim - 1))

    level = one(*pieces[0])
    for cut in pieces[1:]:
        level = level * one(*cut)
    return level


def gaussian(own_key, dims, deviation, bound, shards=(), kind=jnp.bfloat16):
    array = deviation * jax.random.normal(own_key, dims, jnp.float32)
    if shards:
        array = array * block_levels(own_key, dims, shards, -0.22, 0.18)
    return jnp.clip(array, -bound, bound).astype(kind)


def setup_inputs(seed: int = 0, part: int = 0) -> dict:
    keys = jax.random.split(jax.random.key(seed), 4)
    own_keys = jax.random.split(jax.random.fold_in(keys[3], part), 4)
    return {
        "queries": gaussian(own_keys[0], (NQ, K), 1.0, 6.0, ((0, 8),)),
        "whiten": draw_whiten(jax.random.fold_in(jax.random.fold_in(keys[3], part), 71), part),
        "documents": draw_documents(jax.random.fold_in(jax.random.fold_in(keys[3], part), 71), part),
    }


def reference(queries, whiten, documents):
    whitened = jnp.dot(queries, whiten, preferred_element_type=jnp.float32)
    scores = lax.dot_general(whitened, documents, (((1,), (1,)), ((), ())), precision=lax.Precision.HIGHEST, preferred_element_type=jnp.float32)
    count = jnp.float32(NDOC)
    mean = lax.optimization_barrier(jnp.sum(scores, axis=1)) / count
    centered = scores - mean[:, None]
    variance = lax.optimization_barrier(jnp.sum(centered * centered, axis=1)) / count
    return centered * lax.rsqrt(variance + 1e-05)[:, None]
```

```python
import functools
import jax
import jax.numpy as jnp
from jax import lax
from jax.experimental import pallas as pl
from jax.experimental.pallas import tpu as pltpu
from jax.sharding import PartitionSpec as P

F32 = jnp.float32
BF16 = jnp.bfloat16
MESH = pl.DeviceIdType.MESH
NT = (((1,), (1,)), ((), ()))


def from_behind(value, axis, by):
    length = lax.axis_size(axis)
    return lax.ppermute(value, axis, [(i, (i + by) % length) for i in range(length)])


def block_scores(block, documents):
    return lax.dot_general(
        block,
        documents,
        NT,
        precision=lax.Precision.HIGHEST,
        preferred_element_type=jnp.float32,
    )


def ring_plan(queries, whiten, documents):
    q_rows = queries.shape[0]
    n_blk = lax.axis_size("blk")
    n_docs = lax.axis_size("docs")
    here = lax.axis_index("blk")
    core = lax.axis_index("docs")
    span = whiten.shape[0]
    owner_index = here * n_docs + core
    all_queries = lax.all_gather(queries, "blk", axis=0, tiled=True)
    query_cols = lax.dynamic_slice_in_dim(all_queries, owner_index * span, span, 1)
    own_share = lax.psum_scatter(
        jnp.dot(query_cols, whiten, preferred_element_type=jnp.float32),
        ("blk", "docs"),
        scatter_dimension=0,
        tiled=True,
    )
    whitened = lax.all_gather(own_share, "docs", axis=0, tiled=True)

    def place(scores, block, owner):
        return lax.dynamic_update_slice_in_dim(
            scores, block_scores(block, documents), owner * q_rows, 0
        )

    scores = jnp.zeros((q_rows * n_blk, documents.shape[0]), jnp.float32)
    scores = place(scores, whitened, here)

    def step_one(turn, carry):
        held, moving = carry
        moving = from_behind(moving, "blk", 1)
        held = place(held, moving, (here - turn) % n_blk)
        return (held, moving)

    scores, _ = lax.fori_loop(1, n_blk, step_one, (scores, whitened))
    count = jnp.float32(documents.shape[0] * n_blk * n_docs)
    total = lax.psum(jnp.sum(scores, axis=1), ("blk", "docs"))
    mean = total / count
    centered = scores - mean[:, None]
    spread = lax.psum(jnp.sum(centered * centered, axis=1), ("blk", "docs"))
    variance = spread / count
    return centered * lax.rsqrt(variance + 1e-05)[:, None]


def flip(index, mask):
    bit = 1
    while bit <= mask:
        if mask & bit:
            index = index + bit - 2 * bit * ((index // bit) % 2)
        bit *= 2
    return index


def split(value):
    high = value.astype(BF16)
    return high, (value - high.astype(F32)).astype(BF16)


def kernel(
    n_blk,
    q_ref,
    wh_ref,
    d_ref,
    out_ref,
    qbuf,
    whbuf,
    pbuf,
    rbuf,
    ag,
    dbuf,
    dhi,
    dlo,
    stats,
    loc_sem,
    doc_sem,
    q_send,
    q_recv,
    wh_send,
    wh_recv,
    r_send,
    r_recv,
    a_send,
    a_recv,
    f_send,
    f_recv,
    s_send,
    s_recv,
):
    here = lax.axis_index("blk")
    core = lax.axis_index("docs")
    other = 1 - core
    q_rows = q_ref.shape[0]
    depth = qbuf.shape[2]
    wide = pbuf.shape[2]
    half = n_blk * wide
    nq = n_blk * q_rows
    docs = d_ref.shape[0]
    slabs = doc_sem.shape[0]
    slab = docs // slabs
    peers = range(1, n_blk)
    far_first = list(reversed(peers))

    def remote(src, dst, send, recv, blk, docs_index):
        return pltpu.make_async_remote_copy(
            src_ref=src,
            dst_ref=dst,
            send_sem=send,
            recv_sem=recv,
            device_id={"blk": blk, "docs": docs_index},
            device_id_type=MESH,
        )

    def cols(start, size):
        return pl.ds(pl.multiple_of(start, 128), size)

    own_q = pltpu.make_async_copy(
        q_ref.at[:, cols(here * depth, depth)], qbuf.at[here], loc_sem.at[0]
    )
    own_wh = pltpu.make_async_copy(
        wh_ref.at[:, cols(core * half, half)], whbuf.at[core], loc_sem.at[1]
    )
    own_q.start()
    own_wh.start()
    doc_copies = [
        pltpu.make_async_copy(
            d_ref.at[pl.ds(s * slab, slab)], dbuf.at[pl.ds(s * slab, slab)], doc_sem.at[s]
        )
        for s in range(slabs)
    ]
    for copy in doc_copies:
        copy.start()

    barrier = pltpu.get_barrier_semaphore()
    for i in range(n_blk):
        for c in (core, other):
            if i == 0 and c is core:
                continue
            pl.semaphore_signal(
                barrier,
                inc=1,
                device_id={"blk": flip(here, i), "docs": c},
                device_id_type=MESH,
            )
    pl.semaphore_wait(barrier, 2 * n_blk - 1)

    q_copies = {}
    for i in far_first:
        to = flip(here, i)
        q_copies[i] = remote(
            q_ref.at[:, cols(to * depth, depth)],
            qbuf.at[here],
            q_send.at[i],
            q_recv.at[i],
            to,
            core,
        )
        q_copies[i].start()
    wh_copy = remote(
        wh_ref.at[:, cols(other * half, half)],
        whbuf.at[core],
        wh_send,
        wh_recv,
        here,
        other,
    )
    wh_copy.start()

    own_q.wait()
    own_wh.wait()
    wh_copy.wait_recv()
    for i in peers:
        q_copies[i].wait_recv()

    query_cols = qbuf[...].astype(F32).reshape(nq, depth).astype(BF16)
    rows = whbuf[...].reshape(depth, half)
    partial = jnp.dot(query_cols, rows, preferred_element_type=F32)
    for b in range(n_blk):
        pbuf[b] = partial[:, b * wide : (b + 1) * wide]

    r_copies = {}
    for i in far_first:
        to = flip(here, i)
        r_copies[i] = remote(
            pbuf.at[to], rbuf.at[i - 1], r_send.at[i], r_recv.at[i], to, core
        )
        r_copies[i].start()

    step = 32
    for s in range(slabs):
        doc_copies[s].wait()

        def one(t, carry):
            at = pl.ds(pl.multiple_of(s * slab + t * step, step), step)
            for b in range(n_blk):
                for h in range(2):
                    high, low = split(dbuf[at, pl.ds(h * half + b * wide, wide)])
                    dhi[b, at, pl.ds(h * wide, wide)] = high
                    dlo[b, at, pl.ds(h * wide, wide)] = low
            return carry

        lax.fori_loop(0, slab // step, one, 0)

    own = pbuf[here]
    for i in peers:
        r_copies[i].wait_recv()
        own = own + rbuf[i - 1]
    high, low = split(own)
    ag[core, 0, 0:nq] = high
    ag[core, 0, nq : 2 * nq] = low

    def across(i):
        return remote(
            ag.at[core, i], ag.at[core, i], f_send.at[i], f_recv.at[i], here, other
        )

    a_copies = {}
    for i in far_first:
        a_copies[i] = remote(
            ag.at[core, 0], ag.at[core, i], a_send.at[i], a_recv.at[i], flip(here, i), core
        )
        a_copies[i].start()
    f_copies = [across(0)]
    f_copies[0].start()

    for i in range(n_blk):
        if i + 1 < n_blk:
            a_copies[i + 1].wait_recv()
            f_copies.append(across(i + 1))
            f_copies[i + 1].start()
        f_copies[i].wait_recv()
        chunk = flip(here, i)
        left = jnp.concatenate([ag[0, i], ag[1, i]], axis=1)
        both = lax.dot_general(left, dhi[chunk], NT, preferred_element_type=F32)
        term = both[:nq] + both[nq:]
        term += lax.dot_general(left[:nq], dlo[chunk], NT, preferred_element_type=F32)
        if i == 0:
            out_ref[...] = term
        else:
            out_ref[...] += term

    scores = out_ref[...]
    lanes = stats.shape[2]
    eye = lax.broadcasted_iota(jnp.int32, (nq, lanes), 0) == lax.broadcasted_iota(
        jnp.int32, (nq, lanes), 1
    )

    def to_row(column):
        return jnp.sum(jnp.where(eye, column, 0.0), axis=0, keepdims=True)

    def to_column(row):
        return jnp.sum(jnp.where(eye, row, 0.0), axis=1, keepdims=True)

    local_mean = jnp.sum(scores, axis=1, keepdims=True) * (1.0 / docs)
    centered = scores - local_mean
    local_spread = jnp.sum(centered * centered, axis=1, keepdims=True)
    mine = here * 2 + core
    stats[mine, 0:1] = to_row(local_mean)
    stats[mine, 1:2] = to_row(local_spread)
    s_copies = []
    for i in reversed(range(n_blk)):
        for c in (core, other):
            if i == 0 and c is core:
                continue
            k = 2 * i + (0 if c is core else 1)
            copy = remote(
                stats.at[mine],
                stats.at[mine],
                s_send.at[k],
                s_recv.at[k],
                flip(here, i),
                c,
            )
            copy.start()
            s_copies.append(copy)
    for copy in s_copies:
        copy.wait_recv()
    means = stats[:, 0, :]
    spreads = stats[:, 1, :]
    n_dev = 2 * n_blk
    mean = jnp.sum(means, axis=0, keepdims=True) * (1.0 / n_dev)
    away = means - mean
    spread = jnp.sum(spreads + docs * (away * away), axis=0, keepdims=True)
    scale = lax.rsqrt(spread * (1.0 / (docs * n_dev)) + 1e-05)
    out_ref[...] = (scores - to_column(mean)) * to_column(scale)

    for i in peers:
        q_copies[i].wait_send()
        r_copies[i].wait_send()
        a_copies[i].wait_send()
    wh_copy.wait_send()
    for copy in f_copies + s_copies:
        copy.wait_send()


def kernel_plan(queries, whiten, documents):
    n_blk = lax.axis_size("blk")
    q_rows, k = queries.shape
    span = whiten.shape[0]
    docs = documents.shape[0]
    depth = 2 * span
    half = k // 2
    wide = half // n_blk
    nq = q_rows * n_blk
    slabs = 8
    dma = pltpu.SemaphoreType.DMA
    return pl.pallas_call(
        functools.partial(kernel, n_blk),
        out_shape=jax.ShapeDtypeStruct((nq, docs), F32),
        in_specs=[pl.BlockSpec(memory_space=pl.ANY)] * 3,
        out_specs=pl.BlockSpec(memory_space=pltpu.VMEM),
        scratch_shapes=[
            pltpu.VMEM((n_blk, q_rows, depth), BF16),
            pltpu.VMEM((2, span, half), BF16),
            pltpu.VMEM((n_blk, nq, wide), F32),
            pltpu.VMEM((n_blk - 1, nq, wide), F32),
            pltpu.VMEM((2, n_blk, 2 * nq, wide), BF16),
            pltpu.VMEM((docs, k), F32),
            pltpu.VMEM((n_blk, docs, 2 * wide), BF16),
            pltpu.VMEM((n_blk, docs, 2 * wide), BF16),
            pltpu.VMEM((2 * n_blk, 2, 128), F32),
            dma((2,)),
            dma((slabs,)),
            dma((n_blk,)),
            dma((n_blk,)),
            dma,
            dma,
            dma((n_blk,)),
            dma((n_blk,)),
            dma((n_blk,)),
            dma((n_blk,)),
            dma((n_blk,)),
            dma((n_blk,)),
            dma((2 * n_blk,)),
            dma((2 * n_blk,)),
        ],
        compiler_params=pltpu.CompilerParams(
            collective_id=0, has_side_effects=True, vmem_limit_bytes=40 * 2**20
        ),
    )(queries, whiten, documents)


def per_device(queries, whiten, documents):
    n_blk = lax.axis_size("blk")
    q_rows, k = queries.shape
    fits = (
        lax.axis_size("docs") == 2
        and n_blk & (n_blk - 1) == 0
        and n_blk * 2 * whiten.shape[0] == k
        and whiten.shape[0] % 128 == 0
        and k % (256 * n_blk) == 0
        and q_rows % 8 == 0
        and q_rows * n_blk <= 128
        and documents.shape[0] % 256 == 0
        and documents.shape[0] * k <= 2**21
    )
    if fits:
        return kernel_plan(queries, whiten, documents)
    return ring_plan(queries, whiten, documents)


def solution(mesh):
    placed = (
        P(("groups", "blk"), None),
        P(("groups", "blk", "docs"), None),
        P(("groups", "blk", "docs"), None),
    )
    return jax.shard_map(
        per_device,
        mesh=mesh,
        in_specs=placed,
        out_specs=P("groups", ("blk", "docs")),
        check_vma=False,
    )
```

```python
import functools
import jax
import jax.numpy as jnp
from jax import lax
from jax.experimental import pallas as pl
from jax.experimental.pallas import tpu as pltpu
from jax.sharding import PartitionSpec as P

F32 = jnp.float32
BF16 = jnp.bfloat16
MESH = pl.DeviceIdType.MESH
NT = (((1,), (1,)), ((), ()))


def from_behind(value, axis, by):
    length = lax.axis_size(axis)
    return lax.ppermute(value, axis, [(i, (i + by) % length) for i in range(length)])


def block_scores(block, documents):
    return lax.dot_general(
        block,
        documents,
        NT,
        precision=lax.Precision.HIGHEST,
        preferred_element_type=jnp.float32,
    )


def ring_plan(queries, whiten, documents):
    q_rows = queries.shape[0]
    n_blk = lax.axis_size("blk")
    n_docs = lax.axis_size("docs")
    here = lax.axis_index("blk")
    core = lax.axis_index("docs")
    span = whiten.shape[0]
    owner_index = here * n_docs + core
    all_queries = lax.all_gather(queries, "blk", axis=0, tiled=True)
    query_cols = lax.dynamic_slice_in_dim(all_queries, owner_index * span, span, 1)
    own_share = lax.psum_scatter(
        jnp.dot(query_cols, whiten, preferred_element_type=jnp.float32),
        ("blk", "docs"),
        scatter_dimension=0,
        tiled=True,
    )
    whitened = lax.all_gather(own_share, "docs", axis=0, tiled=True)

    def place(scores, block, owner):
        return lax.dynamic_update_slice_in_dim(
            scores, block_scores(block, documents), owner * q_rows, 0
        )

    scores = jnp.zeros((q_rows * n_blk, documents.shape[0]), jnp.float32)
    scores = place(scores, whitened, here)

    def step_one(turn, carry):
        held, moving = carry
        moving = from_behind(moving, "blk", 1)
        held = place(held, moving, (here - turn) % n_blk)
        return (held, moving)

    scores, _ = lax.fori_loop(1, n_blk, step_one, (scores, whitened))
    count = jnp.float32(documents.shape[0] * n_blk * n_docs)
    total = lax.psum(jnp.sum(scores, axis=1), ("blk", "docs"))
    mean = total / count
    centered = scores - mean[:, None]
    spread = lax.psum(jnp.sum(centered * centered, axis=1), ("blk", "docs"))
    variance = spread / count
    return centered * lax.rsqrt(variance + 1e-05)[:, None]


def flip(index, mask):
    bit = 1
    while bit <= mask:
        if mask & bit:
            index = index + bit - 2 * bit * ((index // bit) % 2)
        bit *= 2
    return index


def split(value):
    high = value.astype(BF16)
    return high, (value - high.astype(F32)).astype(BF16)


def kernel(
    n_blk,
    q_ref,
    wh_ref,
    d_ref,
    out_ref,
    qbuf,
    whbuf,
    pbuf,
    rbuf,
    ag,
    dbuf,
    dhi,
    dlo,
    stats,
    loc_sem,
    doc_sem,
    q_send,
    q_recv,
    wh_send,
    wh_recv,
    r_send,
    r_recv,
    a_send,
    a_recv,
    f_send,
    f_recv,
    s_send,
    s_recv,
):
    here = lax.axis_index("blk")
    core = lax.axis_index("docs")
    other = 1 - core
    q_rows = q_ref.shape[0]
    depth = qbuf.shape[2]
    wide = pbuf.shape[2]
    half = n_blk * wide
    nq = n_blk * q_rows
    docs = d_ref.shape[0]
    slabs = doc_sem.shape[0]
    slab = docs // slabs
    peers = range(1, n_blk)
    far_first = list(reversed(peers))

    def remote(src, dst, send, recv, blk, docs_index):
        return pltpu.make_async_remote_copy(
            src_ref=src,
            dst_ref=dst,
            send_sem=send,
            recv_sem=recv,
            device_id={"blk": blk, "docs": docs_index},
            device_id_type=MESH,
        )

    def cols(start, size):
        return pl.ds(pl.multiple_of(start, 128), size)

    own_q = pltpu.make_async_copy(
        q_ref.at[:, cols(here * depth, depth)], qbuf.at[here], loc_sem.at[0]
    )
    own_wh = pltpu.make_async_copy(
        wh_ref.at[:, cols(core * half, half)], whbuf.at[core], loc_sem.at[1]
    )
    own_q.start()
    own_wh.start()
    doc_copies = [
        pltpu.make_async_copy(
            d_ref.at[pl.ds(s * slab, slab)], dbuf.at[pl.ds(s * slab, slab)], doc_sem.at[s]
        )
        for s in range(slabs)
    ]
    for copy in doc_copies:
        copy.start()

    barrier = pltpu.get_barrier_semaphore()
    for i in range(n_blk):
        for c in (core, other):
            if i == 0 and c is core:
                continue
            pl.semaphore_signal(
                barrier,
                inc=1,
                device_id={"blk": flip(here, i), "docs": c},
                device_id_type=MESH,
            )
    pl.semaphore_wait(barrier, 2 * n_blk - 1)

    sends = []
    q_copies = {}
    for i in far_first:
        to = flip(here, i)
        q_copies[i] = remote(
            q_ref.at[:, cols(to * depth, depth)],
            qbuf.at[here],
            q_send.at[i],
            q_recv.at[i],
            to,
            core,
        )
        q_copies[i].start()
        sends.append(q_copies[i])
    wh_copy = remote(
        wh_ref.at[:, cols(other * half, half)],
        whbuf.at[core],
        wh_send,
        wh_recv,
        here,
        other,
    )
    wh_copy.start()
    sends.append(wh_copy)

    own_q.wait()
    own_wh.wait()
    wh_copy.wait_recv()
    for i in peers:
        q_copies[i].wait_recv()

    query_cols = qbuf[...].astype(F32).reshape(nq, depth).astype(BF16)
    rows = whbuf[...].reshape(depth, half)
    partial = jnp.dot(query_cols, rows, preferred_element_type=F32)
    for b in range(n_blk):
        pbuf[b] = partial[:, b * wide : (b + 1) * wide]

    r_copies = {}
    for i in far_first:
        to = flip(here, i)
        r_copies[i] = remote(
            pbuf.at[to], rbuf.at[i - 1], r_send.at[i], r_recv.at[i], to, core
        )
        r_copies[i].start()
        sends.append(r_copies[i])

    step = 32
    for s in range(slabs):
        doc_copies[s].wait()

        def one(t, carry):
            at = pl.ds(pl.multiple_of(s * slab + t * step, step), step)
            for b in range(n_blk):
                for h in range(2):
                    high, low = split(dbuf[at, pl.ds(h * half + b * wide, wide)])
                    dhi[b, at, pl.ds(h * wide, wide)] = high
                    dlo[b, at, pl.ds(h * wide, wide)] = low
            return carry

        lax.fori_loop(0, slab // step, one, 0)

    own = pbuf[here]
    for i in peers:
        r_copies[i].wait_recv()
        own = own + rbuf[i - 1]
    high, low = split(own)
    ag[core, 0, 0:nq] = high
    ag[core, 0, nq : 2 * nq] = low

    def across(i):
        return remote(
            ag.at[core, i], ag.at[core, i], f_send.at[i], f_recv.at[i], here, other
        )

    a_copies = {}
    for i in far_first:
        a_copies[i] = remote(
            ag.at[core, 0], ag.at[core, i], a_send.at[i], a_recv.at[i], flip(here, i), core
        )
        a_copies[i].start()
        sends.append(a_copies[i])
    f_copies = [across(0)]
    f_copies[0].start()

    for i in range(n_blk):
        if i + 1 < n_blk:
            a_copies[i + 1].wait_recv()
            f_copies.append(across(i + 1))
            f_copies[i + 1].start()
        f_copies[i].wait_recv()
        chunk = flip(here, i)
        left = jnp.concatenate([ag[0, i], ag[1, i]], axis=1)
        both = lax.dot_general(left, dhi[chunk], NT, preferred_element_type=F32)
        term = both[:nq] + both[nq:]
        term += lax.dot_general(left[:nq], dlo[chunk], NT, preferred_element_type=F32)
        if i == 0:
            out_ref[...] = term
        else:
            out_ref[...] += term

    scores = out_ref[...]
    lanes = stats.shape[2]
    eye = lax.broadcasted_iota(jnp.int32, (nq, lanes), 0) == lax.broadcasted_iota(
        jnp.int32, (nq, lanes), 1
    )

    def to_row(column):
        return jnp.sum(jnp.where(eye, column, 0.0), axis=0, keepdims=True)

    def to_column(row):
        return jnp.sum(jnp.where(eye, row, 0.0), axis=1, keepdims=True)

    local_mean = jnp.sum(scores, axis=1, keepdims=True) * (1.0 / docs)
    centered = scores - local_mean
    local_spread = jnp.sum(centered * centered, axis=1, keepdims=True)
    mine = here * 2 + core
    stats[mine, 0:1] = to_row(local_mean)
    stats[mine, 1:2] = to_row(local_spread)
    s_copies = []
    for i in reversed(range(n_blk)):
        for c in (core, other):
            if i == 0 and c is core:
                continue
            k = 2 * i + (0 if c is core else 1)
            copy = remote(
                stats.at[mine],
                stats.at[mine],
                s_send.at[k],
                s_recv.at[k],
                flip(here, i),
                c,
            )
            copy.start()
            s_copies.append(copy)
    for copy in s_copies:
        copy.wait_recv()
    means = stats[:, 0, :]
    spreads = stats[:, 1, :]
    n_dev = 2 * n_blk
    mean = jnp.sum(means, axis=0, keepdims=True) * (1.0 / n_dev)
    away = means - mean
    spread = jnp.sum(spreads + docs * (away * away), axis=0, keepdims=True)
    scale = lax.rsqrt(spread * (1.0 / (docs * n_dev)) + 1e-05)
    out_ref[...] = (scores - to_column(mean)) * to_column(scale)

    for copy in sends + f_copies + s_copies:
        copy.wait_send()


def kernel_plan(queries, whiten, documents):
    n_blk = lax.axis_size("blk")
    q_rows, k = queries.shape
    span = whiten.shape[0]
    docs = documents.shape[0]
    depth = 2 * span
    half = k // 2
    wide = half // n_blk
    nq = q_rows * n_blk
    slabs = 8
    dma = pltpu.SemaphoreType.DMA
    return pl.pallas_call(
        functools.partial(kernel, n_blk),
        out_shape=jax.ShapeDtypeStruct((nq, docs), F32),
        in_specs=[pl.BlockSpec(memory_space=pltpu.HBM)] * 3,
        out_specs=pl.BlockSpec(memory_space=pltpu.VMEM),
        scratch_shapes=[
            pltpu.VMEM((n_blk, q_rows, depth), BF16),
            pltpu.VMEM((2, span, half), BF16),
            pltpu.VMEM((n_blk, nq, wide), F32),
            pltpu.VMEM((n_blk - 1, nq, wide), F32),
            pltpu.VMEM((2, n_blk, 2 * nq, wide), BF16),
            pltpu.VMEM((docs, k), F32),
            pltpu.VMEM((n_blk, docs, 2 * wide), BF16),
            pltpu.VMEM((n_blk, docs, 2 * wide), BF16),
            pltpu.VMEM((2 * n_blk, 2, 128), F32),
            dma((2,)),
            dma((slabs,)),
            dma((n_blk,)),
            dma((n_blk,)),
            dma,
            dma,
            dma((n_blk,)),
            dma((n_blk,)),
            dma((n_blk,)),
            dma((n_blk,)),
            dma((n_blk,)),
            dma((n_blk,)),
            dma((2 * n_blk,)),
            dma((2 * n_blk,)),
        ],
        compiler_params=pltpu.CompilerParams(
            collective_id=0, has_side_effects=True, vmem_limit_bytes=64 * 2**20
        ),
    )(queries, whiten, documents)


def per_device(queries, whiten, documents):
    n_blk = lax.axis_size("blk")
    q_rows, k = queries.shape
    fits = (
        lax.axis_size("docs") == 2
        and n_blk & (n_blk - 1) == 0
        and n_blk * 2 * whiten.shape[0] == k
        and whiten.shape[0] % 128 == 0
        and k % (256 * n_blk) == 0
        and q_rows % 8 == 0
        and q_rows * n_blk <= 128
        and documents.shape[0] % 256 == 0
        and documents.shape[0] * k <= 2**21
    )
    if fits:
        return kernel_plan(queries, whiten, documents)
    return ring_plan(queries, whiten, documents)


def solution(mesh):
    placed = (
        P(("groups", "blk"), None),
        P(("groups", "blk", "docs"), None),
        P(("groups", "blk", "docs"), None),
    )
    return jax.shard_map(
        per_device,
        mesh=mesh,
        in_specs=placed,
        out_specs=P("groups", ("blk", "docs")),
        check_vma=False,
    )
```

```python
import functools
import jax
import jax.numpy as jnp
from jax import lax
from jax.experimental import pallas as pl
from jax.experimental.pallas import tpu as pltpu
from jax.sharding import PartitionSpec as P

F32 = jnp.float32
BF16 = jnp.bfloat16
MESH = pl.DeviceIdType.MESH
NT = (((1,), (1,)), ((), ()))


def from_behind(value, axis, by):
    length = lax.axis_size(axis)
    return lax.ppermute(value, axis, [(i, (i + by) % length) for i in range(length)])


def block_scores(block, documents):
    return lax.dot_general(
        block,
        documents,
        NT,
        precision=lax.Precision.HIGHEST,
        preferred_element_type=jnp.float32,
    )


def ring_plan(queries, whiten, documents):
    q_rows = queries.shape[0]
    n_blk = lax.axis_size("blk")
    n_docs = lax.axis_size("docs")
    here = lax.axis_index("blk")
    core = lax.axis_index("docs")
    span = whiten.shape[0]
    owner_index = here * n_docs + core
    all_queries = lax.all_gather(queries, "blk", axis=0, tiled=True)
    query_cols = lax.dynamic_slice_in_dim(all_queries, owner_index * span, span, 1)
    own_share = lax.psum_scatter(
        jnp.dot(query_cols, whiten, preferred_element_type=jnp.float32),
        ("blk", "docs"),
        scatter_dimension=0,
        tiled=True,
    )
    whitened = lax.all_gather(own_share, "docs", axis=0, tiled=True)

    def place(scores, block, owner):
        return lax.dynamic_update_slice_in_dim(
            scores, block_scores(block, documents), owner * q_rows, 0
        )

    scores = jnp.zeros((q_rows * n_blk, documents.shape[0]), jnp.float32)
    scores = place(scores, whitened, here)

    def step_one(turn, carry):
        held, moving = carry
        moving = from_behind(moving, "blk", 1)
        held = place(held, moving, (here - turn) % n_blk)
        return (held, moving)

    scores, _ = lax.fori_loop(1, n_blk, step_one, (scores, whitened))
    count = jnp.float32(documents.shape[0] * n_blk * n_docs)
    total = lax.psum(jnp.sum(scores, axis=1), ("blk", "docs"))
    mean = total / count
    centered = scores - mean[:, None]
    spread = lax.psum(jnp.sum(centered * centered, axis=1), ("blk", "docs"))
    variance = spread / count
    return centered * lax.rsqrt(variance + 1e-05)[:, None]


def flip(index, mask):
    bit = 1
    while bit <= mask:
        if mask & bit:
            index = index + bit - 2 * bit * ((index // bit) % 2)
        bit *= 2
    return index


def split(value):
    high = value.astype(BF16)
    return high, (value - high.astype(F32)).astype(BF16)


def kernel(
    n_blk,
    q_ref,
    wh_ref,
    d_ref,
    out_ref,
    qbuf,
    whbuf,
    pbuf,
    rbuf,
    ag,
    dbuf,
    dhi,
    dlo,
    acc,
    stats,
    loc_sem,
    doc_sem,
    q_send,
    q_recv,
    wh_send,
    wh_recv,
    r_send,
    r_recv,
    a_send,
    a_recv,
    f_send,
    f_recv,
    s_send,
    s_recv,
):
    here = lax.axis_index("blk")
    core = lax.axis_index("docs")
    other = 1 - core
    q_rows = q_ref.shape[0]
    depth = qbuf.shape[2]
    wide = pbuf.shape[2]
    half = n_blk * wide
    nq = n_blk * q_rows
    docs = d_ref.shape[0]
    slabs = doc_sem.shape[0]
    slab = docs // slabs
    peers = range(1, n_blk)
    far_first = list(reversed(peers))

    def remote(src, dst, send, recv, blk, docs_index):
        return pltpu.make_async_remote_copy(
            src_ref=src,
            dst_ref=dst,
            send_sem=send,
            recv_sem=recv,
            device_id={"blk": blk, "docs": docs_index},
            device_id_type=MESH,
        )

    def cols(start, size):
        return pl.ds(pl.multiple_of(start, 128), size)

    own_q = pltpu.make_async_copy(
        q_ref.at[:, cols(here * depth, depth)], qbuf.at[here], loc_sem.at[0]
    )
    own_wh = pltpu.make_async_copy(
        wh_ref.at[:, cols(core * half, half)], whbuf.at[core], loc_sem.at[1]
    )
    own_q.start()
    own_wh.start()
    doc_copies = [
        pltpu.make_async_copy(
            d_ref.at[pl.ds(s * slab, slab)], dbuf.at[pl.ds(s * slab, slab)], doc_sem.at[s]
        )
        for s in range(slabs)
    ]

    barrier = pltpu.get_barrier_semaphore()
    for i in reversed(range(n_blk)):
        for c in (core, other):
            if i == 0 and c is core:
                continue
            pl.semaphore_signal(
                barrier,
                inc=1,
                device_id={"blk": flip(here, i), "docs": c},
                device_id_type=MESH,
            )
    pl.semaphore_wait(barrier, 2 * n_blk - 1)

    sends = []
    q_copies = {}
    for i in far_first:
        to = flip(here, i)
        q_copies[i] = remote(
            q_ref.at[:, cols(to * depth, depth)],
            qbuf.at[here],
            q_send.at[i],
            q_recv.at[i],
            to,
            core,
        )
        q_copies[i].start()
        sends.append(q_copies[i])
    wh_copy = remote(
        wh_ref.at[:, cols(other * half, half)],
        whbuf.at[core],
        wh_send,
        wh_recv,
        here,
        other,
    )
    wh_copy.start()
    sends.append(wh_copy)

    for copy in doc_copies:
        copy.start()

    own_q.wait()
    own_wh.wait()
    wh_copy.wait_recv()
    for i in peers:
        q_copies[i].wait_recv()

    query_cols = qbuf[...].astype(F32).reshape(nq, depth).astype(BF16)
    rows = whbuf[...].reshape(depth, half)
    partial = jnp.dot(query_cols, rows, preferred_element_type=F32)
    for b in range(n_blk):
        pbuf[b] = partial[:, b * wide : (b + 1) * wide]

    def reduce_copy(i, src, to):
        copy = remote(src, rbuf.at[i - 1], r_send.at[i], r_recv.at[i], to, core)
        copy.start()
        sends.append(copy)
        return copy

    r_copies = {}
    for i in (7, 6, 5, 4, 3, 2, 1):
        to = flip(here, i)
        r_copies[i] = reduce_copy(i, pbuf.at[to], to)

    step = 32
    for s in range(slabs):
        doc_copies[s].wait()

        def one(t, carry):
            at = pl.ds(pl.multiple_of(s * slab + t * step, step), step)
            for b in range(n_blk):
                for h in range(2):
                    high, low = split(dbuf[at, pl.ds(h * half + b * wide, wide)])
                    dhi[b, at, pl.ds(h * wide, wide)] = high
                    dlo[b, at, pl.ds(h * wide, wide)] = low
            return carry

        lax.fori_loop(0, slab // step, one, 0)

    own = pbuf[here]
    for i in peers:
        r_copies[i].wait_recv()
        own = own + rbuf[i - 1]
    high, low = split(own)
    ag[core, 0, 0:nq] = high
    ag[core, 0, nq : 2 * nq] = low

    def across(i):
        return remote(
            ag.at[core, i], ag.at[core, i], f_send.at[i], f_recv.at[i], here, other
        )

    def gather_copy(i, src, to):
        copy = remote(ag.at[core, src], ag.at[core, i], a_send.at[i], a_recv.at[i], to, core)
        copy.start()
        sends.append(copy)
        return copy

    a_copies = {i: gather_copy(i, 0, flip(here, i)) for i in (4, 7, 6, 3, 2, 1)}
    f_copies = {0: across(0)}
    f_copies[0].start()

    order = (0, 1, 2, 4, 3, 6, 7, 5)
    for n, i in enumerate(order):
        if n + 1 < n_blk:
            after = order[n + 1]
            a_copies[after].wait_recv()
            if after == 4:
                a_copies[5] = gather_copy(5, 4, flip(here, 1))
            f_copies[after] = across(after)
            f_copies[after].start()
        f_copies[i].wait_recv()
        chunk = flip(here, i)
        left = jnp.concatenate([ag[0, i], ag[1, i]], axis=1)
        both = lax.dot_general(left, dhi[chunk], NT, preferred_element_type=F32)
        term = both[:nq] + both[nq:]
        term += lax.dot_general(left[:nq], dlo[chunk], NT, preferred_element_type=F32)
        if n == 0:
            acc[...] = term
        else:
            acc[...] += term

    scores = acc[...]
    lanes = stats.shape[2]
    eye = lax.broadcasted_iota(jnp.int32, (nq, lanes), 0) == lax.broadcasted_iota(
        jnp.int32, (nq, lanes), 1
    )

    def to_row(column):
        return jnp.sum(jnp.where(eye, column, 0.0), axis=0, keepdims=True)

    def to_column(row):
        return jnp.sum(jnp.where(eye, row, 0.0), axis=1, keepdims=True)

    local_mean = jnp.sum(scores, axis=1, keepdims=True) * (1.0 / docs)
    centered = scores - local_mean
    local_spread = jnp.sum(centered * centered, axis=1, keepdims=True)
    mine = here * 2 + core
    stats[mine, 0:1] = to_row(local_mean)
    stats[mine, 1:2] = to_row(local_spread)
    s_copies = []
    for i in reversed(range(n_blk)):
        for c in (core, other):
            if i == 0 and c is core:
                continue
            k = 2 * i + (0 if c is core else 1)
            copy = remote(
                stats.at[mine],
                stats.at[mine],
                s_send.at[k],
                s_recv.at[k],
                flip(here, i),
                c,
            )
            copy.start()
            s_copies.append(copy)
    for copy in s_copies:
        copy.wait_recv()
    means = stats[:, 0, :]
    spreads = stats[:, 1, :]
    n_dev = 2 * n_blk
    mean = jnp.sum(means, axis=0, keepdims=True) * (1.0 / n_dev)
    away = means - mean
    spread = jnp.sum(spreads + docs * (away * away), axis=0, keepdims=True)
    scale = lax.rsqrt(spread * (1.0 / (docs * n_dev)) + 1e-05)
    out_ref[...] = (scores - to_column(mean)) * to_column(scale)

    for copy in sends + list(f_copies.values()) + s_copies:
        copy.wait_send()


def kernel_plan(queries, whiten, documents):
    n_blk = lax.axis_size("blk")
    q_rows, k = queries.shape
    span = whiten.shape[0]
    docs = documents.shape[0]
    depth = 2 * span
    half = k // 2
    wide = half // n_blk
    nq = q_rows * n_blk
    slabs = 8
    dma = pltpu.SemaphoreType.DMA
    scores = pl.pallas_call(
        functools.partial(kernel, n_blk),
        out_shape=jax.ShapeDtypeStruct((nq, docs), F32),
        in_specs=[pl.BlockSpec(memory_space=pltpu.HBM)] * 3,
        out_specs=pl.BlockSpec(memory_space=pltpu.VMEM),
        scratch_shapes=[
            pltpu.VMEM((n_blk, q_rows, depth), BF16),
            pltpu.VMEM((2, span, half), BF16),
            pltpu.VMEM((n_blk, nq, wide), F32),
            pltpu.VMEM((n_blk - 1, nq, wide), F32),
            pltpu.VMEM((2, n_blk, 2 * nq, wide), BF16),
            pltpu.VMEM((docs, k), F32),
            pltpu.VMEM((n_blk, docs, 2 * wide), BF16),
            pltpu.VMEM((n_blk, docs, 2 * wide), BF16),
            pltpu.VMEM((nq, docs), F32),
            pltpu.VMEM((2 * n_blk, 2, 128), F32),
            dma((2,)),
            dma((slabs,)),
            dma((n_blk,)),
            dma((n_blk,)),
            dma,
            dma,
            dma((n_blk,)),
            dma((n_blk,)),
            dma((n_blk,)),
            dma((n_blk,)),
            dma((n_blk,)),
            dma((n_blk,)),
            dma((2 * n_blk,)),
            dma((2 * n_blk,)),
        ],
        compiler_params=pltpu.CompilerParams(
            collective_id=0, has_side_effects=True, vmem_limit_bytes=64 * 2**20
        ),
    )(queries, whiten, documents)
    return scores


def per_device(queries, whiten, documents):
    n_blk = lax.axis_size("blk")
    q_rows, k = queries.shape
    fits = (
        lax.axis_size("docs") == 2
        and n_blk == 8
        and n_blk * 2 * whiten.shape[0] == k
        and whiten.shape[0] % 128 == 0
        and k % (256 * n_blk) == 0
        and q_rows % 8 == 0
        and q_rows * n_blk <= 128
        and documents.shape[0] % 256 == 0
        and documents.shape[0] * k <= 2**21
    )
    if fits:
        return kernel_plan(queries, whiten, documents)
    return ring_plan(queries, whiten, documents)


def solution(mesh):
    placed = (
        P(("groups", "blk"), None),
        P(("groups", "blk", "docs"), None),
        P(("groups", "blk", "docs"), None),
    )
    return jax.shard_map(
        per_device,
        mesh=mesh,
        in_specs=placed,
        out_specs=P("groups", ("blk", "docs")),
        check_vma=False,
    )
```

```python
import functools
import jax
import jax.numpy as jnp
from jax import lax
from jax.experimental import pallas as pl
from jax.experimental.pallas import tpu as pltpu
from jax.sharding import PartitionSpec as P

F32 = jnp.float32
BF16 = jnp.bfloat16
MESH = pl.DeviceIdType.MESH
NT = (((1,), (1,)), ((), ()))


def from_behind(value, axis, by):
    length = lax.axis_size(axis)
    return lax.ppermute(value, axis, [(i, (i + by) % length) for i in range(length)])


def block_scores(block, documents):
    return lax.dot_general(
        block,
        documents,
        NT,
        precision=lax.Precision.HIGHEST,
        preferred_element_type=jnp.float32,
    )


def ring_plan(queries, whiten, documents):
    q_rows = queries.shape[0]
    n_blk = lax.axis_size("blk")
    n_docs = lax.axis_size("docs")
    here = lax.axis_index("blk")
    core = lax.axis_index("docs")
    span = whiten.shape[0]
    owner_index = here * n_docs + core
    all_queries = lax.all_gather(queries, "blk", axis=0, tiled=True)
    query_cols = lax.dynamic_slice_in_dim(all_queries, owner_index * span, span, 1)
    own_share = lax.psum_scatter(
        jnp.dot(query_cols, whiten, preferred_element_type=jnp.float32),
        ("blk", "docs"),
        scatter_dimension=0,
        tiled=True,
    )
    whitened = lax.all_gather(own_share, "docs", axis=0, tiled=True)

    def place(scores, block, owner):
        return lax.dynamic_update_slice_in_dim(
            scores, block_scores(block, documents), owner * q_rows, 0
        )

    scores = jnp.zeros((q_rows * n_blk, documents.shape[0]), jnp.float32)
    scores = place(scores, whitened, here)

    def step_one(turn, carry):
        held, moving = carry
        moving = from_behind(moving, "blk", 1)
        held = place(held, moving, (here - turn) % n_blk)
        return (held, moving)

    scores, _ = lax.fori_loop(1, n_blk, step_one, (scores, whitened))
    count = jnp.float32(documents.shape[0] * n_blk * n_docs)
    total = lax.psum(jnp.sum(scores, axis=1), ("blk", "docs"))
    mean = total / count
    centered = scores - mean[:, None]
    spread = lax.psum(jnp.sum(centered * centered, axis=1), ("blk", "docs"))
    variance = spread / count
    return centered * lax.rsqrt(variance + 1e-05)[:, None]


def flip(index, mask):
    bit = 1
    while bit <= mask:
        if mask & bit:
            index = index + bit - 2 * bit * ((index // bit) % 2)
        bit *= 2
    return index


def split(value):
    high = value.astype(BF16)
    return high, (value - high.astype(F32)).astype(BF16)


def kernel(
    n_blk,
    q_ref,
    wh_ref,
    d_ref,
    out_ref,
    qbuf,
    whbuf,
    pbuf,
    rbuf,
    ag,
    dbuf,
    dhi,
    dlo,
    acc,
    stats,
    loc_sem,
    doc_sem,
    q_send,
    q_recv,
    wh_send,
    wh_recv,
    r_send,
    r_recv,
    a_send,
    a_recv,
    f_send,
    f_recv,
    s_send,
    s_recv,
):
    here = lax.axis_index("blk")
    core = lax.axis_index("docs")
    other = 1 - core
    q_rows = q_ref.shape[0]
    depth = qbuf.shape[2]
    wide = pbuf.shape[2]
    half = n_blk * wide
    nq = n_blk * q_rows
    docs = d_ref.shape[0]
    slabs = doc_sem.shape[0]
    slab = docs // slabs
    peers = range(1, n_blk)
    far_first = list(reversed(peers))

    def remote(src, dst, send, recv, blk, docs_index):
        return pltpu.make_async_remote_copy(
            src_ref=src,
            dst_ref=dst,
            send_sem=send,
            recv_sem=recv,
            device_id={"blk": blk, "docs": docs_index},
            device_id_type=MESH,
        )

    def cols(start, size):
        return pl.ds(pl.multiple_of(start, 128), size)

    own_q = pltpu.make_async_copy(
        q_ref.at[:, cols(here * depth, depth)], qbuf.at[here], loc_sem.at[0]
    )
    own_wh = pltpu.make_async_copy(
        wh_ref.at[:, cols(core * half, half)], whbuf.at[core], loc_sem.at[1]
    )
    own_q.start()
    own_wh.start()
    doc_copies = [
        pltpu.make_async_copy(
            d_ref.at[pl.ds(s * slab, slab)], dbuf.at[pl.ds(s * slab, slab)], doc_sem.at[s]
        )
        for s in range(slabs)
    ]

    barrier = pltpu.get_barrier_semaphore()
    for i in reversed(range(n_blk)):
        for c in (core, other):
            if i == 0 and c is core:
                continue
            pl.semaphore_signal(
                barrier,
                inc=1,
                device_id={"blk": flip(here, i), "docs": c},
                device_id_type=MESH,
            )
    pl.semaphore_wait(barrier, 2 * n_blk - 1)

    sends = []
    q_copies = {}
    for i in far_first:
        to = flip(here, i)
        q_copies[i] = remote(
            q_ref.at[:, cols(to * depth, depth)],
            qbuf.at[here],
            q_send.at[i],
            q_recv.at[i],
            to,
            core,
        )
        q_copies[i].start()
        sends.append(q_copies[i])
    wh_copy = remote(
        wh_ref.at[:, cols(other * half, half)],
        whbuf.at[core],
        wh_send,
        wh_recv,
        here,
        other,
    )
    wh_copy.start()
    sends.append(wh_copy)

    for copy in doc_copies:
        copy.start()

    own_q.wait()
    own_wh.wait()
    wh_copy.wait_recv()
    for i in peers:
        q_copies[i].wait_recv()

    query_cols = qbuf[...].astype(F32).reshape(nq, depth).astype(BF16)
    rows = whbuf[...].reshape(depth, half)
    partial = jnp.dot(query_cols, rows, preferred_element_type=F32)
    for b in range(n_blk):
        pbuf[b] = partial[:, b * wide : (b + 1) * wide]

    def reduce_copy(i, src, to):
        copy = remote(src, rbuf.at[i - 1], r_send.at[i], r_recv.at[i], to, core)
        copy.start()
        sends.append(copy)
        return copy

    r_copies = {}
    for i in (7, 6, 5, 4, 3, 2, 1):
        to = flip(here, i)
        r_copies[i] = reduce_copy(i, pbuf.at[to], to)

    step = 32
    for s in range(slabs):
        doc_copies[s].wait()

        def one(t, carry):
            at = pl.ds(pl.multiple_of(s * slab + t * step, step), step)
            for b in range(n_blk):
                for h in range(2):
                    high, low = split(dbuf[at, pl.ds(h * half + b * wide, wide)])
                    dhi[b, at, pl.ds(h * wide, wide)] = high
                    dlo[b, at, pl.ds(h * wide, wide)] = low
            return carry

        lax.fori_loop(0, slab // step, one, 0)

    own = pbuf[here]
    for i in peers:
        r_copies[i].wait_recv()
        own = own + rbuf[i - 1]
    high, low = split(own)
    ag[core, 0, 0:nq] = high
    ag[core, 0, nq : 2 * nq] = low

    def across(i):
        return remote(
            ag.at[core, i], ag.at[core, i], f_send.at[i], f_recv.at[i], here, other
        )

    def gather_copy(i, src, to):
        copy = remote(ag.at[core, src], ag.at[core, i], a_send.at[i], a_recv.at[i], to, core)
        copy.start()
        sends.append(copy)
        return copy

    a_copies = {i: gather_copy(i, 0, flip(here, i)) for i in (4, 7, 6, 3, 2, 1)}
    f_copies = {0: across(0)}
    f_copies[0].start()

    order = (0, 1, 4, 2, 3, 6, 7, 5)
    for n, i in enumerate(order):
        if n + 1 < n_blk:
            after = order[n + 1]
            a_copies[after].wait_recv()
            if after == 4:
                a_copies[5] = gather_copy(5, 4, flip(here, 1))
            f_copies[after] = across(after)
            f_copies[after].start()
        f_copies[i].wait_recv()
        chunk = flip(here, i)
        left = jnp.concatenate([ag[0, i], ag[1, i]], axis=1)
        both = lax.dot_general(left, dhi[chunk], NT, preferred_element_type=F32)
        term = both[:nq] + both[nq:]
        term += lax.dot_general(left[:nq], dlo[chunk], NT, preferred_element_type=F32)
        if n == 0:
            acc[...] = term
        else:
            acc[...] += term

    scores = acc[...]
    lanes = stats.shape[2]
    eye = lax.broadcasted_iota(jnp.int32, (nq, lanes), 0) == lax.broadcasted_iota(
        jnp.int32, (nq, lanes), 1
    )

    def to_row(column):
        return jnp.sum(jnp.where(eye, column, 0.0), axis=0, keepdims=True)

    def to_column(row):
        return jnp.sum(jnp.where(eye, row, 0.0), axis=1, keepdims=True)

    local_mean = jnp.sum(scores, axis=1, keepdims=True) * (1.0 / docs)
    centered = scores - local_mean
    local_spread = jnp.sum(centered * centered, axis=1, keepdims=True)
    mine = here * 2 + core
    stats[mine, 0:1] = to_row(local_mean)
    stats[mine, 1:2] = to_row(local_spread)
    s_copies = []
    for i in reversed(range(n_blk)):
        for c in (core, other):
            if i == 0 and c is core:
                continue
            k = 2 * i + (0 if c is core else 1)
            copy = remote(
                stats.at[mine],
                stats.at[mine],
                s_send.at[k],
                s_recv.at[k],
                flip(here, i),
                c,
            )
            copy.start()
            s_copies.append(copy)
    for copy in s_copies:
        copy.wait_recv()
    means = stats[:, 0, :]
    spreads = stats[:, 1, :]
    n_dev = 2 * n_blk
    mean = jnp.sum(means, axis=0, keepdims=True) * (1.0 / n_dev)
    away = means - mean
    spread = jnp.sum(spreads + docs * (away * away), axis=0, keepdims=True)
    scale = lax.rsqrt(spread * (1.0 / (docs * n_dev)) + 1e-05)
    out_ref[...] = (scores - to_column(mean)) * to_column(scale)

    for copy in sends + list(f_copies.values()) + s_copies:
        copy.wait_send()


def kernel_plan(queries, whiten, documents):
    n_blk = lax.axis_size("blk")
    q_rows, k = queries.shape
    span = whiten.shape[0]
    docs = documents.shape[0]
    depth = 2 * span
    half = k // 2
    wide = half // n_blk
    nq = q_rows * n_blk
    slabs = 8
    dma = pltpu.SemaphoreType.DMA
    scores = pl.pallas_call(
        functools.partial(kernel, n_blk),
        out_shape=jax.ShapeDtypeStruct((nq, docs), F32),
        in_specs=[pl.BlockSpec(memory_space=pltpu.HBM)] * 3,
        out_specs=pl.BlockSpec(memory_space=pltpu.VMEM),
        scratch_shapes=[
            pltpu.VMEM((n_blk, q_rows, depth), BF16),
            pltpu.VMEM((2, span, half), BF16),
            pltpu.VMEM((n_blk, nq, wide), F32),
            pltpu.VMEM((n_blk - 1, nq, wide), F32),
            pltpu.VMEM((2, n_blk, 2 * nq, wide), BF16),
            pltpu.VMEM((docs, k), F32),
            pltpu.VMEM((n_blk, docs, 2 * wide), BF16),
            pltpu.VMEM((n_blk, docs, 2 * wide), BF16),
            pltpu.VMEM((nq, docs), F32),
            pltpu.VMEM((2 * n_blk, 2, 128), F32),
            dma((2,)),
            dma((slabs,)),
            dma((n_blk,)),
            dma((n_blk,)),
            dma,
            dma,
            dma((n_blk,)),
            dma((n_blk,)),
            dma((n_blk,)),
            dma((n_blk,)),
            dma((n_blk,)),
            dma((n_blk,)),
            dma((2 * n_blk,)),
            dma((2 * n_blk,)),
        ],
        compiler_params=pltpu.CompilerParams(
            collective_id=0, has_side_effects=True, vmem_limit_bytes=64 * 2**20
        ),
    )(queries, whiten, documents)
    return scores


def per_device(queries, whiten, documents):
    n_blk = lax.axis_size("blk")
    q_rows, k = queries.shape
    fits = (
        lax.axis_size("docs") == 2
        and n_blk == 8
        and n_blk * 2 * whiten.shape[0] == k
        and whiten.shape[0] % 128 == 0
        and k % (256 * n_blk) == 0
        and q_rows % 8 == 0
        and q_rows * n_blk <= 128
        and documents.shape[0] % 256 == 0
        and documents.shape[0] * k <= 2**21
    )
    if fits:
        return kernel_plan(queries, whiten, documents)
    return ring_plan(queries, whiten, documents)


def solution(mesh):
    placed = (
        P(("groups", "blk"), None),
        P(("groups", "blk", "docs"), None),
        P(("groups", "blk", "docs"), None),
    )
    return jax.shard_map(
        per_device,
        mesh=mesh,
        in_specs=placed,
        out_specs=P("groups", ("blk", "docs")),
        check_vma=False,
    )
```
